32 devices in a mesh: grp: 2 (over x), lon: 16 (over z, y, core).
Axes of the slice: x: 2, y: 2, z: 4, core: 2. Of those that a mesh axis runs over, the one named last changes fastest.
Arguments:
- tracers: float32 [64, 4, 96, 256], P('grp', None, 'lon'), parts along dimension 0, may hold values from -6 to 6
- air_mass: float32 [4, 96, 256], P(None, None, 'lon'), may hold values from 1 to 2
- east_flux: float32 [4, 96, 256], P(None, None, 'lon'), may hold values from -0.24 to 0.24, as said below
- north_flux: float32 [4, 96, 256], P(None, None, 'lon'), may hold values from -0.025 to 0.025, as said below
- south_flux: float32 [4, 96], replicated, may hold values from -0.025 to 0.025, as said below
- upward_flux: float32 [3, 96, 256], P(None, None, 'lon'), may hold values from -0.025 to 0.025
- emission: float32 [96, 256], P('lon'), may hold values from 0.5 to 2
- region_map: int32 [96, 256], P('lon'), may hold values from 0 to 31
- limiter_flags: int32 [6], replicated, may hold values 0 or 1
- substep_counts: int32 [256], replicated, may hold values from 1 to 3, as said below
Outputs:
- transported: float32 [64, 4, 96, 256], P('grp', None, 'lon'), parts along dimension 0
- final_mass: float32 [8, 96, 256], P('grp', 'lon'), parts along dimension 0
The draws below stay inside these ranges and needn't reach their ends.
There are 2 independent parts, one for each index of `grp`. The reference program is written for one: setup_inputs(seed, part) draws one part's arguments, and reference() takes and returns one part's arrays. A program takes and returns all parts, laid end to end along the dimension named above; an argument that names none is the same for every part. Nothing has to cross between parts.
Inputs may be any that keep to these rules, and one draw needn't show every extreme that they name: `substep_counts`: the 32 rows nearest each pole have 3 substeps. `east_flux`: the magnitude is at most 0.08 times the substep count of the row. `north_flux`: in the last latitude row (the north pole face) the flux at a longitude is minus the flux 96 / 2 cells away. `south_flux`: the flux at a longitude is minus the flux 96 / 2 cells away.
All inputs are finite; a program needn't handle non-finite values.
Results may differ from the reference program's by a relative error of at most 0.0003.
Values sent between devices are 32-bit elements; how exact they have to be, the bound alone decides.
A program may use at most 64 MiB of HBM per device.

```python
import math
import jax
import jax.numpy as jnp
from jax import lax

TRAC = 32
LAT = 256
LEV = 4
MAXSUB = 3
NLON = 96


def polar_counts(key):
    latitude = jnp.arange(LAT, dtype=jnp.int32)
    chosen = jax.random.randint(jax.random.fold_in(key, 7), (LAT,), 1, MAXSUB + 1, dtype=jnp.int32)
    near_pole = (latitude < LAT // 8) | (latitude >= LAT - LAT // 8)
    return jnp.where(near_pole, MAXSUB, chosen).astype(jnp.int32)


def mirrored(values):
    half_circle = values[..., :NLON // 2]
    return jnp.concatenate([half_circle, -half_circle], axis=-1)


def draw_substep_counts(key, part):
    return polar_counts(key)


def draw_east_flux(key, part):
    counts = polar_counts(key)
    key = jax.random.fold_in(key, 2)
    spread = jax.random.uniform(key, (LEV, NLON, LAT), jnp.float32, -1.0, 1.0)
    return 0.08 * counts.astype(jnp.float32)[None, None, :] * spread


def draw_north_flux(key, part):
    key = jax.random.fold_in(key, 3)
    spread = jax.random.uniform(key, (LEV, NLON, LAT), jnp.float32, -1.0, 1.0)
    spread = spread.at[:, :, LAT - 1].set(mirrored(spread[:, :, LAT - 1]))
    return 0.025 * spread


def draw_south_flux(key, part):
    key = jax.random.fold_in(key, 4)
    spread = jax.random.uniform(key, (LEV, NLON), jnp.float32, -1.0, 1.0)
    return 0.025 * mirrored(spread)


def touch_ends(values, own_key, low, largest):
    shape = values.shape
    index_at = [jax.random.randint(jax.random.fold_in(own_key, axis), (), 0, shape[axis]) for axis in range(len(shape))]
    values = values.at[tuple(index_at)].set(low)
    longest = shape.index(max(shape))
    index_at[longest] = (index_at[longest] + 1) % shape[longest]
    return values.at[tuple(index_at)].set(largest)


def block_scale(key, dims, pieces, least, largest):
    def one(dim, shards_of):
        steps = jax.random.uniform(jax.random.fold_in(jax.random.fold_in(key, 6), dim), (shards_of,), jnp.float32, least / len(pieces), largest / len(pieces))
        return jnp.repeat(jnp.exp(steps), dims[dim] // shards_of).reshape((-1,) + (1,) * (len(dims) - dim - 1))

    level = one(*pieces[0])
    for cut in pieces[1:]:
        level = level * one(*cut)
    return level


def gaussian(stream_key, shape, width, reach, shards=(), kind=jnp.bfloat16):
    result = jax.random.normal(stream_key, shape, jnp.float32) * width
    if len(shards) > 0:
        result = block_scale(stream_key, shape, shards, -0.22, 0.18) * result
    return jnp.clip(result, min=-reach, max=reach).astype(kind)


def setup_inputs(seed: int = 0, part: int = 0) -> dict:
    keys = jax.random.split(jax.random.key(seed), 11)
    own_keys = jax.random.split(jax.random.fold_in(keys[10], part), 11)
    tracers = gaussian(own_keys[0], (TRAC, LEV, NLON, LAT), 1.0, 6.0, ((2, 16),), jnp.float32)
    air_mass = jnp.clip(jnp.exp(math.log(2.0) - 0.6931472 * jax.random.uniform(keys[1], (LEV, NLON, LAT), jnp.float32) ** block_scale(keys[1], (LEV, NLON, LAT), ((2, 16),), -0.2, 0.2)), 1.0, 2.0)
    east_flux = draw_east_flux(jax.random.fold_in(keys[10], 71), part)
    north_flux = draw_north_flux(jax.random.fold_in(keys[10], 71), part)
    south_flux = draw_south_flux(jax.random.fold_in(keys[10], 71), part)
    upward_flux = jnp.clip(jax.random.uniform(keys[5], (LEV - 1, NLON, LAT), jnp.float32, -0.025, 0.025) * block_scale(keys[5], (LEV - 1, NLON, LAT), ((2, 16),), -0.4, 0.0), -0.025, 0.025)
    emission = jnp.clip(jnp.exp(math.log(2.0) - 1.3862944 * jax.random.uniform(keys[6], (NLON, LAT), jnp.float32) ** block_scale(keys[6], (NLON, LAT), ((0, 16),), -0.2, 0.2)), 0.5, 2.0)
    region_map = touch_ends(jax.random.randint(keys[7], (NLON, LAT), 0, TRAC), jax.random.fold_in(keys[7], 1), 0, TRAC - 1).astype(jnp.int32)
    limiter_flags = touch_ends((jax.random.randint(keys[8], (6,), 0, 2) < 1).astype(jnp.int32), jax.random.fold_in(keys[8], 1), 0, 1)
    substep_counts = draw_substep_counts(jax.random.fold_in(keys[10], 71), part)
    return dict(tracers=tracers, air_mass=air_mass, east_flux=east_flux, north_flux=north_flux, south_flux=south_flux, upward_flux=upward_flux, emission=emission, region_map=region_map, limiter_flags=limiter_flags, substep_counts=substep_counts)


sweep_order = "xyzzyx"


def minmod_slopes(ratios, along):
    extent = ratios.shape[along]
    jumps = lax.slice_in_dim(ratios, 1, extent, axis=along) - lax.slice_in_dim(ratios, 0, extent - 1, axis=along)
    number = jumps.shape[along]
    backward = lax.slice_in_dim(jumps, 0, number - 1, axis=along)
    forward = lax.slice_in_dim(jumps, 1, number, axis=along)
    return 0.5 * (jnp.sign(backward) + jnp.sign(forward)) * jnp.minimum(jnp.abs(backward), jnp.abs(forward))


def advect(padded, face_flux, switch, along):
    extent = padded.shape[along] - 4
    air_row = padded[-1:]
    ratios = padded / air_row
    slopes = minmod_slopes(ratios, along) * switch
    ratio_left = lax.slice_in_dim(ratios, 1, extent + 2, axis=along)
    ratio_right = lax.slice_in_dim(ratios, 2, extent + 3, axis=along)
    mass_left = lax.slice_in_dim(air_row, 1, extent + 2, axis=along)
    mass_right = lax.slice_in_dim(air_row, 2, extent + 3, axis=along)
    slope_left = lax.slice_in_dim(slopes, 0, extent + 1, axis=along)
    slope_right = lax.slice_in_dim(slopes, 1, extent + 2, axis=along)
    flowing = face_flux[None]
    from_left = flowing * (ratio_left + 0.5 * (1.0 - flowing / mass_left) * slope_left)
    from_right = flowing * (ratio_right - 0.5 * (1.0 + flowing / mass_right) * slope_right)
    carried = jnp.where(flowing >= 0.0, from_left, from_right)
    inside = lax.slice_in_dim(padded, 2, extent + 2, axis=along)
    return inside - (lax.slice_in_dim(carried, 1, extent + 1, axis=along) - lax.slice_in_dim(carried, 0, extent, axis=along))


def wrap_lon(masses):
    return jnp.concatenate([masses[:, :, -2:], masses, masses[:, :, :2]], axis=2)


def across_poles(masses):
    opposite = jnp.roll(masses, masses.shape[2] // 2, axis=2)
    extent = masses.shape[3]
    return jnp.concatenate([opposite[..., 1:2], opposite[..., 0:1], masses, opposite[..., extent - 1:extent], opposite[..., extent - 2:extent - 1]], axis=3)


def level_edges(masses):
    return jnp.concatenate([masses[:, :1], masses[:, :1], masses, masses[:, -1:], masses[:, -1:]], axis=1)


def transport(masses, switches, counts, pad_x, flux_x, pad_y, flux_y, flux_z):
    portions = 1.0 / counts.astype(jnp.float32)
    for number, direction in enumerate(sweep_order):
        switch = switches[number].astype(jnp.float32)
        if direction == "x":
            for substep in range(MAXSUB):
                active = jnp.where(substep < counts, portions, jnp.zeros_like(portions))
                masses = advect(pad_x(masses), flux_x * active, switch, 2)
        elif direction == "y":
            masses = advect(pad_y(masses), flux_y, switch, 3)
        else:
            masses = advect(level_edges(masses), flux_z, switch, 1)
    return masses


def reference(tracers, air_mass, east_flux, north_flux, south_flux, upward_flux, emission, region_map, limiter_flags, substep_counts):
    labels = jnp.arange(tracers.shape[0], dtype=jnp.int32)
    tagged = (region_map[None] == labels[:, None, None]).astype(jnp.float32)
    surface = tracers[:, 0] + emission[None] * tagged
    seeded = jnp.concatenate([surface[:, None], tracers[:, 1:]], axis=1)
    masses = jnp.concatenate([seeded, air_mass[None]], axis=0)
    flux_x = jnp.concatenate([east_flux[:, -1:], east_flux], axis=1)
    flux_y = jnp.concatenate([south_flux[:, :, None], north_flux], axis=2)
    closed = jnp.zeros((1,) + upward_flux.shape[1:], jnp.float32)
    flux_z = jnp.concatenate([closed, upward_flux, closed], axis=0)
    masses = transport(masses, limiter_flags, substep_counts, wrap_lon, flux_x, across_poles, flux_y, flux_z)
    return masses[:-1], masses[-1]
```

```python
import functools

import jax
import jax.numpy as jnp
from jax import lax
from jax.experimental import pallas as pl
from jax.experimental.pallas import tpu as pltpu
from jax.sharding import PartitionSpec as P

MAXSUB = 3
ROWS = 8
LANES = 128
FIELDS = 16


def minmod(a, b):
    return jnp.maximum(jnp.minimum(a, b), 0.0) + jnp.minimum(jnp.maximum(a, b), 0.0)


def kernel(
    devices,
    levels,
    columns,
    chunks,
    tin,
    spack,
    south,
    scal,
    out,
    mass_out,
    recv,
    field,
    mass,
    inv,
    fx,
    cx,
    fy,
    cy,
    cz,
    hl1,
    hr1,
    hl2,
    hr2,
    state,
    mpack,
    mopp,
    coefs,
    ppack,
    popp,
    f_send,
    f_recv,
    h_send,
    h_recv,
    p_send,
    p_recv,
    m_sem,
):
    me = lax.axis_index("lon")
    right = lax.rem(me + 1, devices)
    left = lax.rem(me + devices - 1, devices)
    opposite = lax.rem(me + devices // 2, devices)
    cells = levels * columns
    lat = tin.shape[-1]
    lat_b = lat // devices
    per_row = LANES // lat_b
    wide = 3 * columns

    def remote(src, dst, send, recv_, to):
        return pltpu.make_async_remote_copy(
            src_ref=src,
            dst_ref=dst,
            send_sem=send,
            recv_sem=recv_,
            device_id={"lon": to},
            device_id_type=pl.DeviceIdType.MESH,
        )

    barrier = pltpu.get_barrier_semaphore()
    for off in range(1, devices):
        pl.semaphore_signal(
            barrier,
            inc=1,
            device_id={"lon": lax.rem(me + off, devices)},
            device_id_type=pl.DeviceIdType.MESH,
        )
    pl.semaphore_wait(barrier, devices - 1)

    def field_copy(off):
        to = lax.rem(me + off, devices)
        return remote(spack.at[to], recv.at[me], f_send.at[off], f_recv.at[off], to)

    def field_wait(off):
        source = lax.rem(me + devices - off, devices)
        return remote(spack.at[source], recv.at[source], f_send.at[off], f_recv.at[off], source)

    for off in range(1, devices):
        field_copy(off).start()

    def to_right(ch, phase):
        src, dst = (tin, hl1) if phase == 0 else (state, hl2)
        return remote(
            src.at[ch], dst.at[ch], h_send.at[phase, 0, ch], h_recv.at[phase, 0, ch], right
        )

    def to_left(ch, phase):
        src, dst = (tin, hr1) if phase == 0 else (state, hr2)
        return remote(
            src.at[ch], dst.at[ch], h_send.at[phase, 1, ch], h_recv.at[phase, 1, ch], left
        )

    for ch in range(chunks):
        to_right(ch, 0).start()
        to_left(ch, 0).start()

    recv[me] = spack[me]
    for off in range(1, devices):
        field_wait(off).wait_recv()

    lane = lax.broadcasted_iota(jnp.int32, (1, LANES), 1)
    lane_lat = lax.broadcasted_iota(jnp.int32, (1, lat), 1)
    first = lane_lat == 0
    final = lane_lat == lat - 1

    for h in range(FIELDS // per_row):

        def unpack(g, carry, h=h):
            for half in range(lat // LANES):
                acc = jnp.zeros((recv.shape[2], LANES), jnp.float32)
                for place in range(per_row):
                    piece = recv[half * per_row + place, h]
                    turned = pltpu.roll(
                        piece, lax.rem(lat_b * (place + per_row - g), LANES), 1
                    )
                    acc = jnp.where(lane // lat_b == place, turned, acc)
                field[g * (FIELDS // per_row) + h, :, half * LANES : (half + 1) * LANES] = acc
            return carry

        lax.fori_loop(0, per_row, unpack, 0)

    def half_switch(number):
        return 0.5 * scal[MAXSUB + number : MAXSUB + number + 1, :]

    def second_order(flux, inv_up, number):
        size = jnp.abs(flux)
        return half_switch(number) * size * (1.0 - size * inv_up)

    tall = field.shape[1]

    def x_air(l, base, number):
        m = mass[base, l]
        r = inv[base, l]
        for k in range(MAXSUB):
            flux = fx[k, l]
            r_next = pltpu.roll(r, tall - 1, 0)
            slot = k if base == 0 else MAXSUB + k
            cx[slot, l] = second_order(flux, jnp.where(flux >= 0.0, r, r_next), number)
            m = m - (flux - pltpu.roll(flux, 1, 0))
            r = 1.0 / m
            mass[base + k + 1, l] = m
            inv[base + k + 1, l] = r

    def y_air(l, base, number, slot):
        m = mass[base, l]
        r = inv[base, l]
        flux = fy[l]
        r_low = pltpu.roll(r, 1, 1)
        cy[slot, l] = second_order(flux, jnp.where(flux >= 0.0, r_low, r), number)
        upper = jnp.where(final, field[2 * levels + l], pltpu.roll(flux, lat - 1, 1))
        m = m - (upper - flux)
        mass[base + 1, l] = m
        inv[base + 1, l] = 1.0 / m

    def z_air(base, number, slot):
        lower = 0.0
        for l in range(levels):
            m = mass[base, l]
            if l < levels - 1:
                upper = field[3 * levels + l]
                cz[slot, l] = second_order(
                    upper, jnp.where(upper >= 0.0, inv[base, l], inv[base, l + 1]), number
                )
                m = m - (upper - lower)
            else:
                m = m + lower
            lower = upper
            mass[base + 1, l] = m
            inv[base + 1, l] = 1.0 / m

    def air_first(l, carry):
        m = field[l]
        mass[0, l] = m
        inv[0, l] = 1.0 / m
        east = field[levels + l]
        for k in range(MAXSUB):
            fx[k, l] = east * scal[k : k + 1, :]
        north = field[2 * levels + l]
        fy[l] = jnp.where(first, south[l], pltpu.roll(north, 1, 1))
        x_air(l, 0, 0)
        y_air(l, 3, 1, 0)
        return carry

    def air_last(l, carry):
        y_air(l, 6, 4, 1)
        x_air(l, 7, 5)
        mass_out[l] = mass[10, l, columns : 2 * columns, :]
        return carry

    lax.fori_loop(0, levels, air_first, 0)
    z_air(4, 2, 0)
    z_air(5, 3, 1)
    lax.fori_loop(0, levels, air_last, 0)

    def place_poles(values, cell, acc):
        ends = jnp.where(lane < LANES // 2, values[:, :LANES], values[:, lat - LANES :])
        ends = jnp.broadcast_to(ends, (ROWS, LANES))
        turned = pltpu.roll(ends, 4 * cell + 2, 1)
        return jnp.where(lane // 4 == cell, turned, acc)

    def air_poles(l, carry):
        accs = list(carry)
        for j in range(columns):
            cell = l * columns + j
            c = columns + j
            accs[0] = place_poles(mass[3, l, c : c + 1, :], cell, accs[0])
            accs[1] = place_poles(mass[6, l, c : c + 1, :], cell, accs[1])
            inflow = jnp.where(
                first, fy[l, c : c + 1, :], -field[2 * levels + l, c : c + 1, :]
            )
            accs[2] = place_poles(inflow, cell, accs[2])
        return tuple(accs)

    nothing = jnp.zeros((ROWS, LANES), jnp.float32)
    packs = lax.fori_loop(0, levels, air_poles, (nothing + 1.0, nothing + 1.0, nothing))
    mpack[0] = packs[0]
    mpack[1] = packs[1]
    inflow = packs[2]
    masses_away = remote(mpack, mopp, m_sem.at[0], m_sem.at[1], opposite)
    masses_away.start()
    masses_away.wait_recv()
    for turn, number in ((0, 1), (1, 4)):
        up = jnp.where(inflow >= 0.0, mopp[turn], mpack[turn])
        size = jnp.abs(inflow)
        coefs[turn] = half_switch(number)[:, :LANES] * size * (1.0 - size / up)
    coefs[2] = inflow

    def row(ref, index, l, c):
        return ref[index, l, c : c + 1, :]

    def x_sub(q, lo, hi, base, slot, k, l, keep):
        jump = {c: q[c] - q[c - 1] for c in range(lo + 1, hi + 1)}
        slope = {c: minmod(jump[c], jump[c + 1]) for c in range(lo + 1, hi)}
        carried = {}
        for c in range(lo + 1, hi - 1):
            flux = row(fx, k, l, c)
            ahead = jnp.broadcast_to(flux, (ROWS, lat)) >= 0.0
            carried[c] = flux * jnp.where(ahead, q[c], q[c + 1]) + row(cx, slot, l, c) * jnp.where(
                ahead, slope[c], slope[c + 1]
            )
        fresh = {}
        for c in range(lo + 2, hi - 1):
            t = row(mass, base, l, c) * q[c] - (carried[c] - carried[c - 1])
            fresh[c] = t if keep else t * row(inv, base + 1, l, c)
        return fresh

    def x_three(q, l, base, slot, keep):
        for k in range(MAXSUB):
            q = x_sub(
                q,
                2 * k,
                wide - 1 - 2 * k,
                base + k,
                slot + k,
                k,
                l,
                keep and k == MAXSUB - 1,
            )
        return q

    def stage_a(ch):
        to_right(ch, 0).wait_recv()
        to_left(ch, 0).wait_recv()

        def level(l, acc):
            q = {}
            for c in range(wide):
                source = (hl1, tin, hr1)[c // columns]
                q[c] = source[ch, l * columns + c % columns] * row(inv, 0, l, c)
            q = x_three(q, l, 0, 0, False)
            for j in range(columns):
                state[ch, l * columns + j] = q[columns + j]
                acc = place_poles(q[columns + j], l * columns + j, acc)
            return acc

        ppack[0, ch] = lax.fori_loop(0, levels, level, nothing)
        poles(ch, 0).start()

    def poles(ch, turn):
        return remote(
            ppack.at[turn, ch],
            popp.at[turn, ch],
            p_send.at[turn, ch],
            p_recv.at[turn, ch],
            opposite,
        )

    def polar(ch, turn):
        poles(ch, turn).wait_recv()
        mine = ppack[turn, ch]
        other = popp[turn, ch]

        def inner(x):
            return jnp.where(lane % 4 == 1, pltpu.roll(x, 1, 1), pltpu.roll(x, LANES - 1, 1))

        across = mine - other
        slope_mine = minmod(across, inner(mine) - mine)
        slope_other = minmod(across, other - inner(other))
        inflow = coefs[2]
        entering = inflow >= 0.0
        carried = inflow * jnp.where(entering, other, mine) + coefs[turn] * jnp.where(
            entering, slope_other, slope_mine
        )
        return across, carried

    def y_level(ch, turn, base, across, carried, l):
        results = []
        for j in range(columns):
            cell = l * columns + j
            back = LANES - 2 - 4 * cell
            edge = pltpu.roll(across, back, 1)
            edge = jnp.concatenate([edge] * (lat // LANES), axis=1)
            enter = pltpu.roll(carried, back, 1)
            enter = jnp.concatenate([enter] * (lat // LANES), axis=1)
            c = columns + j
            q = state[ch, cell]
            low = pltpu.roll(q, 1, 1)
            jump = jnp.where(first, edge, q - low)
            slope = minmod(jump, jnp.where(final, -edge, pltpu.roll(jump, lat - 1, 1)))
            flux = fy[l, c : c + 1, :]
            ahead = jnp.broadcast_to(flux, (ROWS, lat)) >= 0.0
            through = flux * jnp.where(ahead, low, q) + row(cy, turn, l, c) * jnp.where(
                ahead, pltpu.roll(slope, 1, 1), slope
            )
            through = jnp.where(first, enter, through)
            above = jnp.where(final, -enter, pltpu.roll(through, lat - 1, 1))
            results.append(
                (row(mass, base, l, c) * q - (above - through)) * row(inv, base + 1, l, c)
            )
        for j in range(columns):
            state[ch, l * columns + j] = results[j]

    def stage_b(ch):
        across, carried = polar(ch, 0)

        def level(l, carry):
            y_level(ch, 0, 3, across, carried, l)
            return carry

        lax.fori_loop(0, levels, level, 0)
        acc = nothing
        for j in range(columns):
            c = columns + j
            q = [state[ch, l * columns + j] for l in range(levels)]
            for turn in range(2):
                jump = [q[l + 1] - q[l] for l in range(levels - 1)]
                zero = jnp.zeros_like(q[0])
                slope = (
                    [zero]
                    + [minmod(jump[l - 1], jump[l]) for l in range(1, levels - 1)]
                    + [zero]
                )
                carried_up = []
                for l in range(levels - 1):
                    flux = field[3 * levels + l, c : c + 1, :]
                    ahead = jnp.broadcast_to(flux, (ROWS, lat)) >= 0.0
                    carried_up.append(
                        flux * jnp.where(ahead, q[l], q[l + 1])
                        + row(cz, turn, l, c) * jnp.where(ahead, slope[l], slope[l + 1])
                    )
                fresh = []
                for l in range(levels):
                    t = row(mass, 4 + turn, l, c) * q[l]
                    if l < levels - 1:
                        t = t - carried_up[l]
                    if l > 0:
                        t = t + carried_up[l - 1]
                    fresh.append(t * row(inv, 5 + turn, l, c))
                q = fresh
            for l in range(levels):
                state[ch, l * columns + j] = q[l]
                acc = place_poles(q[l], l * columns + j, acc)
        ppack[1, ch] = acc
        poles(ch, 1).start()

    def stage_c(ch):
        across, carried = polar(ch, 1)

        def level(l, carry):
            y_level(ch, 1, 6, across, carried, l)
            return carry

        lax.fori_loop(0, levels, level, 0)
        to_right(ch, 1).start()
        to_left(ch, 1).start()

    def step(i, carry):
        @pl.when(i < chunks)
        def _():
            stage_a(i)

        @pl.when((i >= 1) & (i < chunks + 1))
        def _():
            stage_b(i - 1)

        @pl.when(i >= 2)
        def _():
            stage_c(i - 2)

        return carry

    lax.fori_loop(0, chunks + 2, step, 0)

    def stage_d(ch, carry):
        to_right(ch, 1).wait_recv()
        to_left(ch, 1).wait_recv()

        def level(l, carry):
            q = {}
            for c in range(wide):
                source = (hl2, state, hr2)[c // columns]
                q[c] = source[ch, l * columns + c % columns]
            q = x_three(q, l, 7, MAXSUB, True)
            for j in range(columns):
                out[ch, l * columns + j] = q[columns + j]
            return carry

        lax.fori_loop(0, levels, level, 0)
        return carry

    lax.fori_loop(0, chunks, stage_d, 0)

    for off in range(1, devices):
        field_copy(off).wait_send()
    for ch in range(chunks):
        for phase in range(2):
            to_right(ch, phase).wait_send()
            to_left(ch, phase).wait_send()
            poles(ch, phase).wait_send()
    masses_away.wait_send()


def per_device(
    tracers,
    air_mass,
    east_flux,
    north_flux,
    south_flux,
    upward_flux,
    emission,
    region_map,
    limiter_flags,
    substep_counts,
):
    devices = lax.axis_size("lon")
    position = lax.axis_index("lon")
    count, levels, columns, lat = tracers.shape
    chunks = count // ROWS
    cells = levels * columns
    lat_b = lat // devices
    per_row = LANES // lat_b
    folds = FIELDS // per_row
    tall = -(-3 * columns // 8) * 8

    labels = jnp.arange(count, dtype=jnp.int32)
    tagged = (region_map[None] == labels[:, None, None]).astype(jnp.float32)
    surface = tracers[:, 0] + emission[None] * tagged
    seeded = jnp.concatenate([surface[:, None], tracers[:, 1:]], axis=1)
    tin = seeded.reshape(chunks, ROWS, cells, lat).transpose(0, 2, 1, 3)

    fields = jnp.concatenate([air_mass, east_flux, north_flux, upward_flux], axis=0)
    fields = jnp.pad(fields, ((0, FIELDS - fields.shape[0]), (0, 0), (0, 0)))
    bands = fields.reshape(per_row, folds, devices, columns, lat_b)
    bands = bands.transpose(2, 1, 3, 0, 4).reshape(devices, folds, columns, LANES)
    spack = jnp.concatenate([jnp.roll(bands, 1, 0), bands, jnp.roll(bands, -1, 0)], axis=2)
    spack = jnp.pad(spack, ((0, 0), (0, 0), (0, tall - 3 * columns), (0, 0)))

    doubled = jnp.concatenate([south_flux[:, -columns:], south_flux, south_flux[:, :tall]], axis=1)
    south = lax.dynamic_slice_in_dim(doubled, position * columns, tall, 1)[:, :, None]

    counts = substep_counts.astype(jnp.float32)
    scal = jnp.concatenate(
        [
            jnp.where(
                jnp.arange(MAXSUB)[:, None] < substep_counts[None], 1.0 / counts[None], 0.0
            ),
            jnp.broadcast_to(limiter_flags.astype(jnp.float32)[:, None], (6, lat)),
        ],
        axis=0,
    )

    vmem = functools.partial(pltpu.VMEM, dtype=jnp.float32)
    band = (chunks, cells, ROWS, lat)
    dma = pltpu.SemaphoreType.DMA
    out, final_mass = pl.pallas_call(
        functools.partial(kernel, devices, levels, columns, chunks),
        out_shape=(
            jax.ShapeDtypeStruct(band, jnp.float32),
            jax.ShapeDtypeStruct((levels, columns, lat), jnp.float32),
        ),
        in_specs=[pl.BlockSpec(memory_space=pltpu.VMEM)] * 4,
        out_specs=[pl.BlockSpec(memory_space=pltpu.VMEM)] * 2,
        scratch_shapes=[
            vmem((devices, folds, tall, LANES)),
            vmem((FIELDS, tall, lat)),
            vmem((11, levels, tall, lat)),
            vmem((11, levels, tall, lat)),
            vmem((MAXSUB, levels, tall, lat)),
            vmem((2 * MAXSUB, levels, tall, lat)),
            vmem((levels, tall, lat)),
            vmem((2, levels, tall, lat)),
            vmem((2, levels, tall, lat)),
            vmem(band),
            vmem(band),
            vmem(band),
            vmem(band),
            vmem(band),
            vmem((2, ROWS, LANES)),
            vmem((2, ROWS, LANES)),
            vmem((3, ROWS, LANES)),
            vmem((2, chunks, ROWS, LANES)),
            vmem((2, chunks, ROWS, LANES)),
            dma((devices,)),
            dma((devices,)),
            dma((2, 2, chunks)),
            dma((2, 2, chunks)),
            dma((2, chunks)),
            dma((2, chunks)),
            dma((2,)),
        ],
        compiler_params=pltpu.CompilerParams(
            collective_id=0, has_side_effects=True, vmem_limit_bytes=40 * 2**20
        ),
    )(tin, spack, south, scal)
    transported = (
        out.reshape(chunks, cells, ROWS, lat)
        .transpose(0, 2, 1, 3)
        .reshape(count, levels, columns, lat)
    )
    return transported, final_mass


def solution(mesh):
    return jax.shard_map(
        per_device,
        mesh=mesh,
        in_specs=(
            P("grp", None, "lon", None),
            P(None, None, "lon"),
            P(None, None, "lon"),
            P(None, None, "lon"),
            P(),
            P(None, None, "lon"),
            P("lon", None),
            P("lon", None),
            P(),
            P(),
        ),
        out_specs=(P("grp", None, "lon", None), P("grp", "lon", None)),
        check_vma=False,
    )
```

```python
import functools

import jax
import jax.numpy as jnp
from jax import lax
from jax.experimental import pallas as pl
from jax.experimental.pallas import tpu as pltpu
from jax.sharding import PartitionSpec as P

MAXSUB = 3
ROWS = 8
LANES = 128
FIELDS = 16


def minmod(a, b):
    return jnp.maximum(jnp.minimum(a, b), 0.0) + jnp.minimum(jnp.maximum(a, b), 0.0)


def kernel(
    devices,
    levels,
    columns,
    chunks,
    tin,
    air_in,
    east_in,
    north_in,
    up_in,
    south_in,
    counts_in,
    flags_in,
    out,
    mass_out,
    gather,
    around,
    spack,
    south,
    scal,
    recv,
    field,
    mass,
    inv,
    fx,
    cx,
    fy,
    cy,
    cz,
    hl1,
    hr1,
    hl2,
    hr2,
    state,
    mpack,
    mopp,
    coefs,
    ppack,
    popp,
    f_send,
    f_recv,
    h_send,
    h_recv,
    p_send,
    p_recv,
    m_sem,
):
    me = lax.axis_index("lon")
    right = lax.rem(me + 1, devices)
    left = lax.rem(me + devices - 1, devices)
    opposite = lax.rem(me + devices // 2, devices)
    cells = levels * columns
    lat = tin.shape[-1]
    lat_b = lat // devices
    per_row = LANES // lat_b
    wide = 3 * columns
    total = columns * devices

    def remote(src, dst, send, recv_, to):
        return pltpu.make_async_remote_copy(
            src_ref=src,
            dst_ref=dst,
            send_sem=send,
            recv_sem=recv_,
            device_id={"lon": to},
            device_id_type=pl.DeviceIdType.MESH,
        )

    barrier = pltpu.get_barrier_semaphore()
    for off in range(1, devices):
        pl.semaphore_signal(
            barrier,
            inc=1,
            device_id={"lon": lax.rem(me + off, devices)},
            device_id_type=pl.DeviceIdType.MESH,
        )
    pl.semaphore_wait(barrier, devices - 1)

    def to_right(ch, phase):
        src, dst = (tin, hl1) if phase == 0 else (state, hl2)
        return remote(
            src.at[ch], dst.at[ch], h_send.at[phase, 0, ch], h_recv.at[phase, 0, ch], right
        )

    def to_left(ch, phase):
        src, dst = (tin, hr1) if phase == 0 else (state, hr2)
        return remote(
            src.at[ch], dst.at[ch], h_send.at[phase, 1, ch], h_recv.at[phase, 1, ch], left
        )

    for ch in range(chunks):
        to_right(ch, 0).start()
        to_left(ch, 0).start()

    def field_copy(off):
        to = lax.rem(me + off, devices)
        return remote(spack.at[to], recv.at[me], f_send.at[off], f_recv.at[off], to)

    def field_wait(off):
        source = lax.rem(me + devices - off, devices)
        return remote(spack.at[source], recv.at[source], f_send.at[off], f_recv.at[off], source)

    gather[...] = jnp.zeros_like(gather)
    place = 0
    for source in (air_in, east_in, north_in, up_in):
        for l in range(source.shape[0]):
            gather[place * lat_b : (place + 1) * lat_b, :total] = source[l]
            place += 1
    for h in range(FIELDS // per_row):
        turned = gather[h * LANES : (h + 1) * LANES, :].T
        around[h, 0:columns, :] = turned[total - columns : total]
        around[h, columns : columns + total, :] = turned[:total]
        around[h, columns + total : 2 * columns + total, :] = turned[:columns]
    for to in range(devices):
        for h in range(FIELDS // per_row):
            spack[to, h, :wide, :] = around[h, to * columns : to * columns + wide, :]
            spack[to, h, wide:, :] = jnp.ones((spack.shape[2] - wide, LANES), jnp.float32)

    for off in range(1, devices):
        field_copy(off).start()

    counts = counts_in[...]
    portion = 1.0 / counts.astype(jnp.float32)
    for k in range(MAXSUB):
        scal[k : k + 1, :] = jnp.where(k < counts, portion, 0.0)
    for n in range(6):
        scal[MAXSUB + n : MAXSUB + n + 1, :] = jnp.full(
            (1, lat), flags_in[n].astype(jnp.float32), jnp.float32
        )
    tall = field.shape[1]
    here = lax.broadcasted_iota(jnp.int32, (tall, total), 1)
    want = lax.rem(
        lax.broadcasted_iota(jnp.int32, (tall, total), 0) + me * columns + total - columns, total
    )
    for l in range(levels):
        south[l] = jnp.sum(
            jnp.where(here == want, south_in[l : l + 1, :], 0.0), axis=1, keepdims=True
        )

    recv[me] = spack[me]
    for off in range(1, devices):
        field_wait(off).wait_recv()

    lane = lax.broadcasted_iota(jnp.int32, (1, LANES), 1)
    lane_lat = lax.broadcasted_iota(jnp.int32, (1, lat), 1)
    first = lane_lat == 0
    final = lane_lat == lat - 1

    for h in range(FIELDS // per_row):

        def unpack(g, carry, h=h):
            for half in range(lat // LANES):
                acc = jnp.zeros((recv.shape[2], LANES), jnp.float32)
                for place in range(per_row):
                    piece = recv[half * per_row + place, h]
                    turned = pltpu.roll(
                        piece, lax.rem(lat_b * (place + per_row - g), LANES), 1
                    )
                    acc = jnp.where(lane // lat_b == place, turned, acc)
                field[h * per_row + g, :, half * LANES : (half + 1) * LANES] = acc
            return carry

        lax.fori_loop(0, per_row, unpack, 0)

    def half_switch(number):
        return 0.5 * scal[MAXSUB + number : MAXSUB + number + 1, :]

    def second_order(flux, inv_up, number):
        size = jnp.abs(flux)
        return half_switch(number) * size * (1.0 - size * inv_up)

    def x_air(l, base, number):
        m = mass[base, l]
        r = inv[base, l]
        for k in range(MAXSUB):
            flux = fx[k, l]
            r_next = pltpu.roll(r, tall - 1, 0)
            slot = k if base == 0 else MAXSUB + k
            cx[slot, l] = second_order(flux, jnp.where(flux >= 0.0, r, r_next), number)
            m = m - (flux - pltpu.roll(flux, 1, 0))
            r = 1.0 / m
            mass[base + k + 1, l] = m
            inv[base + k + 1, l] = r

    def y_air(l, base, number, slot):
        m = mass[base, l]
        r = inv[base, l]
        flux = fy[l]
        r_low = pltpu.roll(r, 1, 1)
        cy[slot, l] = second_order(flux, jnp.where(flux >= 0.0, r_low, r), number)
        upper = jnp.where(final, field[2 * levels + l], pltpu.roll(flux, lat - 1, 1))
        m = m - (upper - flux)
        mass[base + 1, l] = m
        inv[base + 1, l] = 1.0 / m

    def z_air(base, number, slot):
        lower = 0.0
        for l in range(levels):
            m = mass[base, l]
            if l < levels - 1:
                upper = field[3 * levels + l]
                cz[slot, l] = second_order(
                    upper, jnp.where(upper >= 0.0, inv[base, l], inv[base, l + 1]), number
                )
                m = m - (upper - lower)
            else:
                m = m + lower
            lower = upper
            mass[base + 1, l] = m
            inv[base + 1, l] = 1.0 / m

    def air_first(l, carry):
        m = field[l]
        mass[0, l] = m
        inv[0, l] = 1.0 / m
        east = field[levels + l]
        for k in range(MAXSUB):
            fx[k, l] = east * scal[k : k + 1, :]
        north = field[2 * levels + l]
        fy[l] = jnp.where(first, south[l], pltpu.roll(north, 1, 1))
        x_air(l, 0, 0)
        y_air(l, 3, 1, 0)
        return carry

    def air_last(l, carry):
        y_air(l, 6, 4, 1)
        x_air(l, 7, 5)
        mass_out[l] = mass[10, l, columns : 2 * columns, :]
        return carry

    lax.fori_loop(0, levels, air_first, 0)
    z_air(4, 2, 0)
    z_air(5, 3, 1)
    lax.fori_loop(0, levels, air_last, 0)

    def place_poles(values, cell, acc):
        ends = jnp.where(lane < LANES // 2, values[:, :LANES], values[:, lat - LANES :])
        ends = jnp.broadcast_to(ends, (ROWS, LANES))
        turned = pltpu.roll(ends, 4 * cell + 2, 1)
        return jnp.where(lane // 4 == cell, turned, acc)

    def air_poles(l, carry):
        accs = list(carry)
        for j in range(columns):
            cell = l * columns + j
            c = columns + j
            accs[0] = place_poles(mass[3, l, c : c + 1, :], cell, accs[0])
            accs[1] = place_poles(mass[6, l, c : c + 1, :], cell, accs[1])
            inflow = jnp.where(
                first, fy[l, c : c + 1, :], -field[2 * levels + l, c : c + 1, :]
            )
            accs[2] = place_poles(inflow, cell, accs[2])
        return tuple(accs)

    nothing = jnp.zeros((ROWS, LANES), jnp.float32)
    packs = lax.fori_loop(0, levels, air_poles, (nothing + 1.0, nothing + 1.0, nothing))
    mpack[0] = packs[0]
    mpack[1] = packs[1]
    inflow = packs[2]
    masses_away = remote(mpack, mopp, m_sem.at[0], m_sem.at[1], opposite)
    masses_away.start()
    masses_away.wait_recv()
    for turn, number in ((0, 1), (1, 4)):
        up = jnp.where(inflow >= 0.0, mopp[turn], mpack[turn])
        size = jnp.abs(inflow)
        coefs[turn] = half_switch(number)[:, :LANES] * size * (1.0 - size / up)
    coefs[2] = inflow

    def row(ref, index, l, c):
        return ref[index, l, c : c + 1, :]

    def x_sub(q, lo, hi, base, slot, k, l, keep):
        jump = {c: q[c] - q[c - 1] for c in range(lo + 1, hi + 1)}
        slope = {c: minmod(jump[c], jump[c + 1]) for c in range(lo + 1, hi)}
        carried = {}
        for c in range(lo + 1, hi - 1):
            flux = row(fx, k, l, c)
            ahead = jnp.broadcast_to(flux, (ROWS, lat)) >= 0.0
            carried[c] = flux * jnp.where(ahead, q[c], q[c + 1]) + row(cx, slot, l, c) * jnp.where(
                ahead, slope[c], slope[c + 1]
            )
        fresh = {}
        for c in range(lo + 2, hi - 1):
            t = row(mass, base, l, c) * q[c] - (carried[c] - carried[c - 1])
            fresh[c] = t if keep else t * row(inv, base + 1, l, c)
        return fresh

    def x_three(q, l, base, slot, keep):
        for k in range(MAXSUB):
            q = x_sub(
                q,
                2 * k,
                wide - 1 - 2 * k,
                base + k,
                slot + k,
                k,
                l,
                keep and k == MAXSUB - 1,
            )
        return q

    def stage_a(ch):
        to_right(ch, 0).wait_recv()
        to_left(ch, 0).wait_recv()

        def level(l, acc):
            q = {}
            for c in range(wide):
                source = (hl1, tin, hr1)[c // columns]
                q[c] = source[ch, l * columns + c % columns] * row(inv, 0, l, c)
            q = x_three(q, l, 0, 0, False)
            for j in range(columns):
                state[ch, l * columns + j] = q[columns + j]
                acc = place_poles(q[columns + j], l * columns + j, acc)
            return acc

        ppack[0, ch] = lax.fori_loop(0, levels, level, nothing)
        poles(ch, 0).start()

    def poles(ch, turn):
        return remote(
            ppack.at[turn, ch],
            popp.at[turn, ch],
            p_send.at[turn, ch],
            p_recv.at[turn, ch],
            opposite,
        )

    def polar(ch, turn):
        poles(ch, turn).wait_recv()
        mine = ppack[turn, ch]
        other = popp[turn, ch]

        def inner(x):
            return jnp.where(lane % 4 == 1, pltpu.roll(x, 1, 1), pltpu.roll(x, LANES - 1, 1))

        across = mine - other
        slope_mine = minmod(across, inner(mine) - mine)
        slope_other = minmod(across, other - inner(other))
        inflow = coefs[2]
        entering = inflow >= 0.0
        carried = inflow * jnp.where(entering, other, mine) + coefs[turn] * jnp.where(
            entering, slope_other, slope_mine
        )
        return across, carried

    def y_level(ch, turn, base, across, carried, l):
        results = []
        for j in range(columns):
            cell = l * columns + j
            back = LANES - 2 - 4 * cell
            edge = pltpu.roll(across, back, 1)
            edge = jnp.concatenate([edge] * (lat // LANES), axis=1)
            enter = pltpu.roll(carried, back, 1)
            enter = jnp.concatenate([enter] * (lat // LANES), axis=1)
            c = columns + j
            q = state[ch, cell]
            low = pltpu.roll(q, 1, 1)
            jump = jnp.where(first, edge, q - low)
            slope = minmod(jump, jnp.where(final, -edge, pltpu.roll(jump, lat - 1, 1)))
            flux = fy[l, c : c + 1, :]
            ahead = jnp.broadcast_to(flux, (ROWS, lat)) >= 0.0
            through = flux * jnp.where(ahead, low, q) + row(cy, turn, l, c) * jnp.where(
                ahead, pltpu.roll(slope, 1, 1), slope
            )
            through = jnp.where(first, enter, through)
            above = jnp.where(final, -enter, pltpu.roll(through, lat - 1, 1))
            results.append(
                (row(mass, base, l, c) * q - (above - through)) * row(inv, base + 1, l, c)
            )
        for j in range(columns):
            state[ch, l * columns + j] = results[j]

    def stage_b(ch):
        across, carried = polar(ch, 0)

        for l in range(levels):
            y_level(ch, 0, 3, across, carried, l)
        acc = nothing
        for j in range(columns):
            c = columns + j
            q = [state[ch, l * columns + j] for l in range(levels)]
            for turn in range(2):
                jump = [q[l + 1] - q[l] for l in range(levels - 1)]
                zero = jnp.zeros_like(q[0])
                slope = (
                    [zero]
                    + [minmod(jump[l - 1], jump[l]) for l in range(1, levels - 1)]
                    + [zero]
                )
                carried_up = []
                for l in range(levels - 1):
                    flux = field[3 * levels + l, c : c + 1, :]
                    ahead = jnp.broadcast_to(flux, (ROWS, lat)) >= 0.0
                    carried_up.append(
                        flux * jnp.where(ahead, q[l], q[l + 1])
                        + row(cz, turn, l, c) * jnp.where(ahead, slope[l], slope[l + 1])
                    )
                fresh = []
                for l in range(levels):
                    t = row(mass, 4 + turn, l, c) * q[l]
                    if l < levels - 1:
                        t = t - carried_up[l]
                    if l > 0:
                        t = t + carried_up[l - 1]
                    fresh.append(t * row(inv, 5 + turn, l, c))
                q = fresh
            for l in range(levels):
                state[ch, l * columns + j] = q[l]
                acc = place_poles(q[l], l * columns + j, acc)
        ppack[1, ch] = acc
        poles(ch, 1).start()

    def stage_c(ch):
        across, carried = polar(ch, 1)

        for l in range(levels):
            y_level(ch, 1, 6, across, carried, l)
        to_right(ch, 1).start()
        to_left(ch, 1).start()

    def step(i, carry):
        @pl.when(i >= 2)
        def _():
            stage_c(i - 2)

        @pl.when((i >= 1) & (i < chunks + 1))
        def _():
            stage_b(i - 1)

        @pl.when(i < chunks)
        def _():
            stage_a(i)

        return carry

    lax.fori_loop(0, chunks + 2, step, 0)

    def stage_d(ch, carry):
        to_right(ch, 1).wait_recv()
        to_left(ch, 1).wait_recv()

        def level(l, carry):
            q = {}
            for c in range(wide):
                source = (hl2, state, hr2)[c // columns]
                q[c] = source[ch, l * columns + c % columns]
            q = x_three(q, l, 7, MAXSUB, True)
            for j in range(columns):
                out[ch, l * columns + j] = q[columns + j]
            return carry

        lax.fori_loop(0, levels, level, 0)
        return carry

    lax.fori_loop(0, chunks, stage_d, 0)

    for off in range(1, devices):
        field_copy(off).wait_send()
    for ch in range(chunks):
        for phase in range(2):
            to_right(ch, phase).wait_send()
            to_left(ch, phase).wait_send()
            poles(ch, phase).wait_send()
    masses_away.wait_send()


def per_device(
    tracers,
    air_mass,
    east_flux,
    north_flux,
    south_flux,
    upward_flux,
    emission,
    region_map,
    limiter_flags,
    substep_counts,
):
    devices = lax.axis_size("lon")
    count, levels, columns, lat = tracers.shape
    chunks = count // ROWS
    cells = levels * columns
    lat_b = lat // devices
    per_row = LANES // lat_b
    folds = FIELDS // per_row
    tall = -(-3 * columns // 8) * 8

    labels = jnp.arange(count, dtype=jnp.int32)
    tagged = (region_map[None] == labels[:, None, None]).astype(jnp.float32)
    surface = tracers[:, 0] + emission[None] * tagged
    seeded = jnp.concatenate([surface[:, None], tracers[:, 1:]], axis=1)
    tin = seeded.reshape(chunks, ROWS, cells, lat).transpose(0, 2, 1, 3)

    turned = [x.transpose(0, 2, 1) for x in (air_mass, east_flux, north_flux, upward_flux)]
    total = columns * devices
    padded = -(-total // LANES) * LANES

    vmem = functools.partial(pltpu.VMEM, dtype=jnp.float32)
    band = (chunks, cells, ROWS, lat)
    dma = pltpu.SemaphoreType.DMA
    out, final_mass = pl.pallas_call(
        functools.partial(kernel, devices, levels, columns, chunks),
        out_shape=(
            jax.ShapeDtypeStruct(band, jnp.float32),
            jax.ShapeDtypeStruct((levels, columns, lat), jnp.float32),
        ),
        in_specs=[pl.BlockSpec(memory_space=pltpu.VMEM)] * 7
        + [pl.BlockSpec(memory_space=pltpu.SMEM)],
        out_specs=[pl.BlockSpec(memory_space=pltpu.VMEM)] * 2,
        scratch_shapes=[
            vmem((FIELDS * lat_b, padded)),
            vmem((folds, -(-(total + 2 * columns) // 8) * 8, LANES)),
            vmem((devices, folds, tall, LANES)),
            vmem((levels, tall, 1)),
            vmem((16, lat)),
            vmem((devices, folds, tall, LANES)),
            vmem((FIELDS, tall, lat)),
            vmem((11, levels, tall, lat)),
            vmem((11, levels, tall, lat)),
            vmem((MAXSUB, levels, tall, lat)),
            vmem((2 * MAXSUB, levels, tall, lat)),
            vmem((levels, tall, lat)),
            vmem((2, levels, tall, lat)),
            vmem((2, levels, tall, lat)),
            vmem(band),
            vmem(band),
            vmem(band),
            vmem(band),
            vmem(band),
            vmem((2, ROWS, LANES)),
            vmem((2, ROWS, LANES)),
            vmem((3, ROWS, LANES)),
            vmem((2, chunks, ROWS, LANES)),
            vmem((2, chunks, ROWS, LANES)),
            dma((devices,)),
            dma((devices,)),
            dma((2, 2, chunks)),
            dma((2, 2, chunks)),
            dma((2, chunks)),
            dma((2, chunks)),
            dma((2,)),
        ],
        compiler_params=pltpu.CompilerParams(
            collective_id=0, has_side_effects=True, vmem_limit_bytes=40 * 2**20
        ),
    )(tin, *turned, south_flux, substep_counts[None], limiter_flags)
    transported = (
        out.reshape(chunks, cells, ROWS, lat)
        .transpose(0, 2, 1, 3)
        .reshape(count, levels, columns, lat)
    )
    return transported, final_mass


def solution(mesh):
    return jax.shard_map(
        per_device,
        mesh=mesh,
        in_specs=(
            P("grp", None, "lon", None),
            P(None, None, "lon"),
            P(None, None, "lon"),
            P(None, None, "lon"),
            P(),
            P(None, None, "lon"),
            P("lon", None),
            P("lon", None),
            P(),
            P(),
        ),
        out_specs=(P("grp", None, "lon", None), P("grp", "lon", None)),
        check_vma=False,
    )
```

```python
import functools

import jax
import jax.numpy as jnp
from jax import lax
from jax.experimental import pallas as pl
from jax.experimental.pallas import tpu as pltpu
from jax.sharding import PartitionSpec as P

MAXSUB = 3
AHEAD = 2
ROWS = 8
LANES = 128
FIELDS = 16


def minmod(a, b):
    return jnp.maximum(jnp.minimum(a, b), 0.0) + jnp.minimum(jnp.maximum(a, b), 0.0)


def kernel(
    devices,
    levels,
    columns,
    chunks,
    tin,
    air_in,
    east_in,
    north_in,
    up_in,
    south_in,
    counts_in,
    flags_in,
    out,
    mass_out,
    gather,
    around,
    spack,
    south,
    scal,
    recv,
    field,
    mass,
    inv,
    fx,
    cx,
    fy,
    cy,
    cz,
    hl1,
    hr1,
    hl2,
    hr2,
    state,
    mpack,
    mopp,
    coefs,
    ppack,
    popp,
    f_send,
    f_recv,
    h_send,
    h_recv,
    p_send,
    p_recv,
    m_sem,
):
    me = lax.axis_index("lon")
    right = lax.rem(me + 1, devices)
    left = lax.rem(me + devices - 1, devices)
    opposite = lax.rem(me + devices // 2, devices)
    cells = levels * columns
    lat = tin.shape[-1]
    lat_b = lat // devices
    per_row = LANES // lat_b
    wide = 3 * columns
    total = columns * devices

    def remote(src, dst, send, recv_, to):
        return pltpu.make_async_remote_copy(
            src_ref=src,
            dst_ref=dst,
            send_sem=send,
            recv_sem=recv_,
            device_id={"lon": to},
            device_id_type=pl.DeviceIdType.MESH,
        )

    barrier = pltpu.get_barrier_semaphore()
    for off in range(1, devices):
        pl.semaphore_signal(
            barrier,
            inc=1,
            device_id={"lon": lax.rem(me + off, devices)},
            device_id_type=pl.DeviceIdType.MESH,
        )
    pl.semaphore_wait(barrier, devices - 1)

    def to_right(ch, phase):
        src, dst = (tin, hl1) if phase == 0 else (state, hl2)
        return remote(
            src.at[ch], dst.at[ch], h_send.at[phase, 0, ch], h_recv.at[phase, 0, ch], right
        )

    def to_left(ch, phase):
        src, dst = (tin, hr1) if phase == 0 else (state, hr2)
        return remote(
            src.at[ch], dst.at[ch], h_send.at[phase, 1, ch], h_recv.at[phase, 1, ch], left
        )

    def field_copy(off):
        to = lax.rem(me + off, devices)
        return remote(spack.at[to], recv.at[me], f_send.at[off], f_recv.at[off], to)

    def field_wait(off):
        source = lax.rem(me + devices - off, devices)
        return remote(spack.at[source], recv.at[source], f_send.at[off], f_recv.at[off], source)

    gather[...] = jnp.zeros_like(gather)
    place = 0
    for source in (air_in, east_in, north_in, up_in):
        for l in range(source.shape[0]):
            gather[place * lat_b : (place + 1) * lat_b, :total] = source[l]
            place += 1
    for h in range(FIELDS // per_row):
        turned = gather[h * LANES : (h + 1) * LANES, :].T
        around[h, 0:columns, :] = turned[total - columns : total]
        around[h, columns : columns + total, :] = turned[:total]
        around[h, columns + total : 2 * columns + total, :] = turned[:columns]
    for to in range(devices):
        for h in range(FIELDS // per_row):
            spack[to, h, :wide, :] = around[h, to * columns : to * columns + wide, :]
            spack[to, h, wide:, :] = jnp.ones((spack.shape[2] - wide, LANES), jnp.float32)

    for off in range(1, devices):
        field_copy(off).start()
    for ch in range(1):
        to_right(ch, 0).start()
        to_left(ch, 0).start()

    counts = counts_in[...]
    portion = 1.0 / counts.astype(jnp.float32)
    for k in range(MAXSUB):
        scal[k : k + 1, :] = jnp.where(k < counts, portion, 0.0)
    for n in range(6):
        scal[MAXSUB + n : MAXSUB + n + 1, :] = jnp.full(
            (1, lat), flags_in[n].astype(jnp.float32), jnp.float32
        )
    tall = field.shape[1]
    here = lax.broadcasted_iota(jnp.int32, (tall, total), 1)
    want = lax.rem(
        lax.broadcasted_iota(jnp.int32, (tall, total), 0) + me * columns + total - columns, total
    )
    for l in range(levels):
        south[l] = jnp.sum(
            jnp.where(here == want, south_in[l : l + 1, :], 0.0), axis=1, keepdims=True
        )

    recv[me] = spack[me]
    for off in range(1, devices):
        field_wait(off).wait_recv()
    for ch in range(1, AHEAD):
        to_right(ch, 0).start()
        to_left(ch, 0).start()

    lane = lax.broadcasted_iota(jnp.int32, (1, LANES), 1)
    lane_lat = lax.broadcasted_iota(jnp.int32, (1, lat), 1)
    first = lane_lat == 0
    final = lane_lat == lat - 1

    for h in range(FIELDS // per_row):

        def unpack(g, carry, h=h):
            for half in range(lat // LANES):
                acc = jnp.zeros((recv.shape[2], LANES), jnp.float32)
                for place in range(per_row):
                    piece = recv[half * per_row + place, h]
                    turned = pltpu.roll(
                        piece, lax.rem(lat_b * (place + per_row - g), LANES), 1
                    )
                    acc = jnp.where(lane // lat_b == place, turned, acc)
                field[h * per_row + g, :, half * LANES : (half + 1) * LANES] = acc
            return carry

        lax.fori_loop(0, per_row, unpack, 0)

    def half_switch(number):
        return 0.5 * scal[MAXSUB + number : MAXSUB + number + 1, :]

    def second_order(flux, inv_up, number):
        size = jnp.abs(flux)
        return half_switch(number) * size * (1.0 - size * inv_up)

    def x_air(l, base, number):
        m = mass[base, l]
        r = inv[base, l]
        for k in range(MAXSUB):
            flux = fx[k, l]
            r_next = pltpu.roll(r, tall - 1, 0)
            slot = k if base == 0 else MAXSUB + k
            cx[slot, l] = second_order(flux, jnp.where(flux >= 0.0, r, r_next), number)
            m = m - (flux - pltpu.roll(flux, 1, 0))
            r = 1.0 / m
            mass[base + k + 1, l] = m
            inv[base + k + 1, l] = r

    def y_air(l, base, number, slot):
        m = mass[base, l]
        r = inv[base, l]
        flux = fy[l]
        r_low = pltpu.roll(r, 1, 1)
        cy[slot, l] = second_order(flux, jnp.where(flux >= 0.0, r_low, r), number)
        upper = jnp.where(final, field[2 * levels + l], pltpu.roll(flux, lat - 1, 1))
        m = m - (upper - flux)
        mass[base + 1, l] = m
        inv[base + 1, l] = 1.0 / m

    def z_air(base, number, slot):
        lower = 0.0
        for l in range(levels):
            m = mass[base, l]
            if l < levels - 1:
                upper = field[3 * levels + l]
                cz[slot, l] = second_order(
                    upper, jnp.where(upper >= 0.0, inv[base, l], inv[base, l + 1]), number
                )
                m = m - (upper - lower)
            else:
                m = m + lower
            lower = upper
            mass[base + 1, l] = m
            inv[base + 1, l] = 1.0 / m

    def air_first(l, carry):
        m = field[l]
        mass[0, l] = m
        inv[0, l] = 1.0 / m
        east = field[levels + l]
        for k in range(MAXSUB):
            fx[k, l] = east * scal[k : k + 1, :]
        north = field[2 * levels + l]
        fy[l] = jnp.where(first, south[l], pltpu.roll(north, 1, 1))
        x_air(l, 0, 0)
        y_air(l, 3, 1, 0)
        return carry

    def air_last(l, carry):
        y_air(l, 6, 4, 1)
        x_air(l, 7, 5)
        mass_out[l] = mass[10, l, columns : 2 * columns, :]
        return carry

    lax.fori_loop(0, levels, air_first, 0)
    z_air(4, 2, 0)
    z_air(5, 3, 1)
    lax.fori_loop(0, levels, air_last, 0)

    def place_poles(values, cell, acc):
        ends = jnp.where(lane < LANES // 2, values[:, :LANES], values[:, lat - LANES :])
        ends = jnp.broadcast_to(ends, (ROWS, LANES))
        turned = pltpu.roll(ends, 4 * cell + 2, 1)
        return jnp.where(lane // 4 == cell, turned, acc)

    def air_poles(l, carry):
        accs = list(carry)
        for j in range(columns):
            cell = l * columns + j
            c = columns + j
            accs[0] = place_poles(mass[3, l, c : c + 1, :], cell, accs[0])
            accs[1] = place_poles(mass[6, l, c : c + 1, :], cell, accs[1])
            inflow = jnp.where(
                first, fy[l, c : c + 1, :], -field[2 * levels + l, c : c + 1, :]
            )
            accs[2] = place_poles(inflow, cell, accs[2])
        return tuple(accs)

    nothing = jnp.zeros((ROWS, LANES), jnp.float32)
    packs = lax.fori_loop(0, levels, air_poles, (nothing + 1.0, nothing + 1.0, nothing))
    mpack[0] = packs[0]
    mpack[1] = packs[1]
    inflow = packs[2]
    masses_away = remote(mpack, mopp, m_sem.at[0], m_sem.at[1], opposite)
    masses_away.start()
    masses_away.wait_recv()
    for turn, number in ((0, 1), (1, 4)):
        up = jnp.where(inflow >= 0.0, mopp[turn], mpack[turn])
        size = jnp.abs(inflow)
        coefs[turn] = half_switch(number)[:, :LANES] * size * (1.0 - size / up)
    coefs[2] = inflow

    def row(ref, index, l, c):
        return ref[index, l, c : c + 1, :]

    def x_sub(q, lo, hi, base, slot, k, l, keep):
        jump = {c: q[c] - q[c - 1] for c in range(lo + 1, hi + 1)}
        slope = {c: minmod(jump[c], jump[c + 1]) for c in range(lo + 1, hi)}
        carried = {}
        for c in range(lo + 1, hi - 1):
            flux = row(fx, k, l, c)
            ahead = jnp.broadcast_to(flux, (ROWS, lat)) >= 0.0
            carried[c] = flux * jnp.where(ahead, q[c], q[c + 1]) + row(cx, slot, l, c) * jnp.where(
                ahead, slope[c], slope[c + 1]
            )
        fresh = {}
        for c in range(lo + 2, hi - 1):
            t = row(mass, base, l, c) * q[c] - (carried[c] - carried[c - 1])
            fresh[c] = t if keep else t * row(inv, base + 1, l, c)
        return fresh

    def x_three(q, l, base, slot, keep):
        for k in range(MAXSUB):
            q = x_sub(
                q,
                2 * k,
                wide - 1 - 2 * k,
                base + k,
                slot + k,
                k,
                l,
                keep and k == MAXSUB - 1,
            )
        return q

    def stage_a(ch):
        to_right(ch, 0).wait_recv()
        to_left(ch, 0).wait_recv()

        def level(l, acc):
            q = {}
            for c in range(wide):
                source = (hl1, tin, hr1)[c // columns]
                q[c] = source[ch, l * columns + c % columns] * row(inv, 0, l, c)
            q = x_three(q, l, 0, 0, False)
            for j in range(columns):
                state[ch, l * columns + j] = q[columns + j]
                acc = place_poles(q[columns + j], l * columns + j, acc)
            return acc

        ppack[0, ch] = lax.fori_loop(0, levels, level, nothing)
        poles(ch, 0).start()

    def poles(ch, turn):
        return remote(
            ppack.at[turn, ch],
            popp.at[turn, ch],
            p_send.at[turn, ch],
            p_recv.at[turn, ch],
            opposite,
        )

    def polar(ch, turn):
        poles(ch, turn).wait_recv()
        mine = ppack[turn, ch]
        other = popp[turn, ch]

        def inner(x):
            return jnp.where(lane % 4 == 1, pltpu.roll(x, 1, 1), pltpu.roll(x, LANES - 1, 1))

        across = mine - other
        slope_mine = minmod(across, inner(mine) - mine)
        slope_other = minmod(across, other - inner(other))
        inflow = coefs[2]
        entering = inflow >= 0.0
        carried = inflow * jnp.where(entering, other, mine) + coefs[turn] * jnp.where(
            entering, slope_other, slope_mine
        )
        return across, carried

    def y_level(ch, turn, base, across, carried, l):
        results = []
        for j in range(columns):
            cell = l * columns + j
            back = LANES - 2 - 4 * cell
            edge = pltpu.roll(across, back, 1)
            edge = jnp.concatenate([edge] * (lat // LANES), axis=1)
            enter = pltpu.roll(carried, back, 1)
            enter = jnp.concatenate([enter] * (lat // LANES), axis=1)
            c = columns + j
            q = state[ch, cell]
            low = pltpu.roll(q, 1, 1)
            jump = jnp.where(first, edge, q - low)
            slope = minmod(jump, jnp.where(final, -edge, pltpu.roll(jump, lat - 1, 1)))
            flux = fy[l, c : c + 1, :]
            ahead = jnp.broadcast_to(flux, (ROWS, lat)) >= 0.0
            through = flux * jnp.where(ahead, low, q) + row(cy, turn, l, c) * jnp.where(
                ahead, pltpu.roll(slope, 1, 1), slope
            )
            through = jnp.where(first, enter, through)
            above = jnp.where(final, -enter, pltpu.roll(through, lat - 1, 1))
            results.append(
                (row(mass, base, l, c) * q - (above - through)) * row(inv, base + 1, l, c)
            )
        for j in range(columns):
            state[ch, l * columns + j] = results[j]

    def stage_b(ch):
        across, carried = polar(ch, 0)

        for l in range(levels):
            y_level(ch, 0, 3, across, carried, l)
        acc = nothing
        for j in range(columns):
            c = columns + j
            q = [state[ch, l * columns + j] for l in range(levels)]
            for turn in range(2):
                jump = [q[l + 1] - q[l] for l in range(levels - 1)]
                zero = jnp.zeros_like(q[0])
                slope = (
                    [zero]
                    + [minmod(jump[l - 1], jump[l]) for l in range(1, levels - 1)]
                    + [zero]
                )
                carried_up = []
                for l in range(levels - 1):
                    flux = field[3 * levels + l, c : c + 1, :]
                    ahead = jnp.broadcast_to(flux, (ROWS, lat)) >= 0.0
                    carried_up.append(
                        flux * jnp.where(ahead, q[l], q[l + 1])
                        + row(cz, turn, l, c) * jnp.where(ahead, slope[l], slope[l + 1])
                    )
                fresh = []
                for l in range(levels):
                    t = row(mass, 4 + turn, l, c) * q[l]
                    if l < levels - 1:
                        t = t - carried_up[l]
                    if l > 0:
                        t = t + carried_up[l - 1]
                    fresh.append(t * row(inv, 5 + turn, l, c))
                q = fresh
            for l in range(levels):
                state[ch, l * columns + j] = q[l]
                acc = place_poles(q[l], l * columns + j, acc)
        ppack[1, ch] = acc
        poles(ch, 1).start()

    def stage_c(ch):
        across, carried = polar(ch, 1)

        for l in range(levels):
            y_level(ch, 1, 6, across, carried, l)
        to_right(ch, 1).start()
        to_left(ch, 1).start()

    def step(i, carry):
        @pl.when((i >= 1) & (i < chunks + 1))
        def _():
            stage_b(i - 1)

        @pl.when(i < chunks)
        def _():
            stage_a(i)

        @pl.when(i < chunks - AHEAD)
        def _():
            to_right(i + AHEAD, 0).start()
            to_left(i + AHEAD, 0).start()

        @pl.when(i >= 2)
        def _():
            stage_c(i - 2)

        return carry

    lax.fori_loop(0, chunks + 2, step, 0)

    def stage_d(ch, carry):
        to_right(ch, 1).wait_recv()
        to_left(ch, 1).wait_recv()

        def level(l, carry):
            q = {}
            for c in range(wide):
                source = (hl2, state, hr2)[c // columns]
                q[c] = source[ch, l * columns + c % columns]
            q = x_three(q, l, 7, MAXSUB, True)
            for j in range(columns):
                out[ch, l * columns + j] = q[columns + j]
            return carry

        lax.fori_loop(0, levels, level, 0)
        return carry

    lax.fori_loop(0, chunks, stage_d, 0)

    for off in range(1, devices):
        field_copy(off).wait_send()
    for ch in range(chunks):
        for phase in range(2):
            to_right(ch, phase).wait_send()
            to_left(ch, phase).wait_send()
            poles(ch, phase).wait_send()
    masses_away.wait_send()


def per_device(
    tracers,
    air_mass,
    east_flux,
    north_flux,
    south_flux,
    upward_flux,
    emission,
    region_map,
    limiter_flags,
    substep_counts,
):
    devices = lax.axis_size("lon")
    count, levels, columns, lat = tracers.shape
    chunks = count // ROWS
    cells = levels * columns
    lat_b = lat // devices
    per_row = LANES // lat_b
    folds = FIELDS // per_row
    tall = -(-3 * columns // 8) * 8

    labels = jnp.arange(count, dtype=jnp.int32)
    tagged = (region_map[None] == labels[:, None, None]).astype(jnp.float32)
    surface = tracers[:, 0] + emission[None] * tagged
    seeded = jnp.concatenate([surface[:, None], tracers[:, 1:]], axis=1)
    tin = seeded.reshape(chunks, ROWS, cells, lat).transpose(0, 2, 1, 3)

    turned = [x.transpose(0, 2, 1) for x in (air_mass, east_flux, north_flux, upward_flux)]
    total = columns * devices
    padded = -(-total // LANES) * LANES

    vmem = functools.partial(pltpu.VMEM, dtype=jnp.float32)
    band = (chunks, cells, ROWS, lat)
    dma = pltpu.SemaphoreType.DMA
    out, final_mass = pl.pallas_call(
        functools.partial(kernel, devices, levels, columns, chunks),
        out_shape=(
            jax.ShapeDtypeStruct(band, jnp.float32),
            jax.ShapeDtypeStruct((levels, columns, lat), jnp.float32),
        ),
        in_specs=[pl.BlockSpec(memory_space=pltpu.VMEM)] * 7
        + [pl.BlockSpec(memory_space=pltpu.SMEM)],
        out_specs=[pl.BlockSpec(memory_space=pltpu.VMEM)] * 2,
        scratch_shapes=[
            vmem((FIELDS * lat_b, padded)),
            vmem((folds, -(-(total + 2 * columns) // 8) * 8, LANES)),
            vmem((devices, folds, tall, LANES)),
            vmem((levels, tall, 1)),
            vmem((16, lat)),
            vmem((devices, folds, tall, LANES)),
            vmem((FIELDS, tall, lat)),
            vmem((11, levels, tall, lat)),
            vmem((11, levels, tall, lat)),
            vmem((MAXSUB, levels, tall, lat)),
            vmem((2 * MAXSUB, levels, tall, lat)),
            vmem((levels, tall, lat)),
            vmem((2, levels, tall, lat)),
            vmem((2, levels, tall, lat)),
            vmem(band),
            vmem(band),
            vmem(band),
            vmem(band),
            vmem(band),
            vmem((2, ROWS, LANES)),
            vmem((2, ROWS, LANES)),
            vmem((3, ROWS, LANES)),
            vmem((2, chunks, ROWS, LANES)),
            vmem((2, chunks, ROWS, LANES)),
            dma((devices,)),
            dma((devices,)),
            dma((2, 2, chunks)),
            dma((2, 2, chunks)),
            dma((2, chunks)),
            dma((2, chunks)),
            dma((2,)),
        ],
        compiler_params=pltpu.CompilerParams(
            collective_id=0, has_side_effects=True, vmem_limit_bytes=40 * 2**20
        ),
    )(tin, *turned, south_flux, substep_counts[None], limiter_flags)
    transported = (
        out.reshape(chunks, cells, ROWS, lat)
        .transpose(0, 2, 1, 3)
        .reshape(count, levels, columns, lat)
    )
    return transported, final_mass


def solution(mesh):
    return jax.shard_map(
        per_device,
        mesh=mesh,
        in_specs=(
            P("grp", None, "lon", None),
            P(None, None, "lon"),
            P(None, None, "lon"),
            P(None, None, "lon"),
            P(),
            P(None, None, "lon"),
            P("lon", None),
            P("lon", None),
            P(),
            P(),
        ),
        out_specs=(P("grp", None, "lon", None), P("grp", "lon", None)),
        check_vma=False,
    )
```
